512 devices in a mesh: section: 4 (over y_lo, core), ctx: 16 (over z), head: 8 (over x, y_hi).
Axes of the slice: x: 4, y: 4 (y_hi: 2, y_lo: 2; y = y_hi * 2 + y_lo), z: 16, core: 2. Of those that a mesh axis runs over, the one named last changes fastest.
Arguments:
- self_hidden: bfloat16 [8192, 4096], P(('section', 'ctx')), may hold values from -6 to 6
- kv_weight: bfloat16 [4096, 2048], P('section', 'head'), may hold values from -0.09375 to 0.09375
- signs: int32 [8, 128], P('head'), may hold values from -1 to 1, as said below
- positions: int32 [8192], replicated, may hold values from 0 to 8191, as said below
- queries: bfloat16 [8192, 4096], P(('section', 'ctx'), 'head'), may hold values from -112 to 112
- out_weight: bfloat16 [4096, 4096], P('head', 'section'), may hold values from -0.375 to 0.375
- query_weight: bfloat16 [4096, 4096], P('section', 'head'), may hold values from -0.09375 to 0.09375
- norm_gain: bfloat16 [4096], replicated, may hold values from 0.099609375 to 1.8984375
Outputs:
- stream: bfloat16 [8192, 4096], P(('section', 'ctx'), 'head')
- second: bfloat16 [8192, 4096], P(('section', 'ctx'), 'head')
The draws below stay inside these ranges and needn't reach their ends.
Inputs may be any that keep to these rules, and one draw needn't show every extreme that they name: `signs`: every entry is -1 or +1. Within each aligned block of 128 tokens the positions rise by one; every position from 0 to 8191 appears exactly once.
All inputs are finite; a program needn't handle non-finite values.
Results may differ from the reference program's by a relative error of at most 0.035.
Values may be sent and summed in bfloat16 or wider, within the bound.
No kernel may reach another device: no remote copies, remote signals or barrier semaphores. Data moves between devices by JAX's collectives and lax.ppermute only.
A program may use at most 64 MiB of HBM per device.

```python
import math
import jax
import jax.numpy as jnp
from jax import lax

D = 4096
HEADS = 32
KVH = 8
HD = 128
TOK_DEV = 128
TOKENS = 8192


def draw_signs(key, part):
    key = jax.random.fold_in(key, 11)
    coins = jax.random.randint(key, (KVH, HD), 0, 2, dtype=jnp.int32)
    return 2 * coins - 1


def draw_positions(key, part):
    key = jax.random.fold_in(key, 12)
    block_order = jax.random.permutation(key, TOKENS // TOK_DEV).astype(jnp.int32)
    within = jnp.arange(TOKENS, dtype=jnp.int32) % TOK_DEV
    return jnp.repeat(block_order, TOK_DEV, total_repeat_length=TOKENS) * TOK_DEV + within


def draw_queries(key, part):
    key = jax.random.fold_in(key, 13)
    normal_base = jax.random.normal(key, (TOKENS, HEADS * HD), jnp.float32)
    return jnp.clip(normal_base, -6.0, 6.0).astype(jnp.bfloat16)


def block_levels(key, extent, shards, least, high):
    gain = 1.0
    for position, shards_of in shards:
        heights = jax.random.uniform(jax.random.fold_in(jax.random.fold_in(key, 6), position), (shards_of,), jnp.float32, least / len(shards), high / len(shards))
        gain = gain * jnp.repeat(jnp.exp(heights), extent[position] // shards_of).reshape((-1,) + (1,) * (len(extent) - 1 - position))
    return gain


def scatter_about(key, dims, deviation, limit, shards=(), kind=jnp.bfloat16):
    gain = block_levels(key, dims, shards, -0.22, 0.18) if shards else 1.0
    drawn = jax.random.normal(key, dims, jnp.float32) * deviation * gain
    return jnp.minimum(jnp.maximum(drawn, -limit), limit).astype(kind)


def setup_inputs(seed: int = 0) -> dict:
    seeds = jax.random.split(jax.random.key(seed), 9)
    self_hidden = scatter_about(seeds[0], (TOKENS, D), 1.0, 6.0, ((0, 64),))
    kv_weight = scatter_about(seeds[1], (D, KVH * 2 * HD), D ** -0.5, 0.09375, ((0, 4), (1, 8)))
    signs = draw_signs(jax.random.fold_in(seeds[8], 71), 0)
    positions = draw_positions(jax.random.fold_in(seeds[8], 71), 0)
    queries = draw_queries(jax.random.fold_in(seeds[8], 71), 0)
    out_weight = scatter_about(seeds[5], (HEADS * HD, D), (HEADS * HD // 16) ** -0.5, 0.375, ((0, 8), (1, 4)))
    query_weight = scatter_about(seeds[6], (D, HEADS * HD), D ** -0.5, 0.09375, ((0, 4), (1, 8)))
    norm_gain = jnp.clip(1.0 + 0.18 * jax.random.normal(seeds[7], (D,), jnp.float32), 0.099609375, 1.8984375).astype(jnp.bfloat16)
    return dict(self_hidden=self_hidden, kv_weight=kv_weight, signs=signs, positions=positions, queries=queries, out_weight=out_weight, query_weight=query_weight, norm_gain=norm_gain)


def hadamard_table():
    indices = jnp.arange(HD, dtype=jnp.int32)
    intersection = jnp.bitwise_and(indices[:, None], indices[None, :])
    parity = jnp.zeros((HD, HD), jnp.int32)
    for bit_index in range(HD.bit_length() - 1):
        parity = parity + jnp.bitwise_and(jnp.right_shift(intersection, bit_index), 1)
    parity = jnp.bitwise_and(parity, 1)
    return (1.0 - 2.0 * parity.astype(jnp.float32)) * jnp.float32(1.0 / math.sqrt(HD))

def rotated_cache(self_hidden, kv_weight, signs):
    projected = jnp.dot(self_hidden, kv_weight, preferred_element_type=jnp.float32)
    projected = projected.reshape(TOKENS, KVH, 2, HD) * signs.astype(jnp.float32)[None, :, None, :]
    rotated = jnp.einsum('tkcd,de->tkce', projected, hadamard_table(), precision=lax.Precision.HIGHEST)
    return rotated.astype(jnp.bfloat16)

def cross_attention(query_rows, cache, positions):
    group_size = HEADS // KVH
    block_rows = TOK_DEV
    block_count = TOKENS // block_rows
    query_heads = query_rows.reshape(block_count, block_rows, KVH, group_size, HD).astype(jnp.float32)
    query_pos = positions.reshape(block_count, block_rows)
    key_rows = cache[:, :, 0, :].astype(jnp.float32)
    value_rows = cache[:, :, 1, :].astype(jnp.float32)
    inv_root = jnp.float32(1.0 / math.sqrt(HD))

    def one_block(inputs):
        query_block, pos_block = inputs
        scores = jnp.einsum('bkgd,skd->kgbs', query_block, key_rows) * inv_root
        allowed = positions[None, :] <= pos_block[:, None]
        scores = jnp.where(allowed[None, None], scores, -jnp.inf)
        highest = lax.optimization_barrier(jnp.max(scores, axis=-1, keepdims=True))
        weights = jnp.exp(scores - highest)
        denominator = lax.optimization_barrier(jnp.sum(weights, axis=-1))
        rounded = lax.optimization_barrier(weights.astype(jnp.bfloat16)).astype(jnp.float32)
        attended = jnp.einsum('kgbs,skd->bkgd', rounded, value_rows)
        return attended / jnp.transpose(denominator, (2, 0, 1))[..., None]
    result = lax.map(one_block, (query_heads, query_pos))
    return result.reshape(TOKENS, HEADS * HD).astype(jnp.bfloat16)

def reference(self_hidden, kv_weight, signs, positions, queries, out_weight, query_weight, norm_gain):
    cache = rotated_cache(self_hidden, kv_weight, signs)
    first_layer = cross_attention(queries, cache, positions)
    residual_sum = self_hidden.astype(jnp.float32) + jnp.dot(first_layer, out_weight, preferred_element_type=jnp.float32)
    mean_square = lax.optimization_barrier(jnp.mean(residual_sum * residual_sum, axis=-1, keepdims=True))
    normed = (residual_sum * lax.rsqrt(mean_square + 1e-06) * norm_gain.astype(jnp.float32)).astype(jnp.bfloat16)
    second_queries = jnp.dot(normed, query_weight, preferred_element_type=jnp.float32).astype(jnp.bfloat16)
    second = cross_attention(second_queries, cache, positions)
    return (residual_sum.astype(jnp.bfloat16), second)
```

```python
import functools
import math

import jax
import jax.numpy as jnp
from jax import lax
from jax.experimental import pallas as pl
from jax.experimental.pallas import tpu as pltpu
from jax.sharding import PartitionSpec as P

HD = 128
KV = 2 * HD
TAIL = 16
VMEM_LIMIT = 48 * 2**20

SMEM_SPEC = pl.BlockSpec(memory_space=pltpu.SMEM)
VMEM_SPEC = pl.BlockSpec(memory_space=pltpu.VMEM)


def dot(a, b):
    return jnp.dot(a, b, preferred_element_type=jnp.float32)


def kv_partial_kernel(section, hidden, from_near, from_far, weight, mate_weight, own, near):
    depth = weight.shape[0]
    here = section[0]
    mine = hidden[:, pl.ds(pl.multiple_of(here * depth, depth), depth)]
    mates = hidden[:, pl.ds(pl.multiple_of((here ^ 1) * depth, depth), depth)]
    rows = mine.shape[0]
    both = dot(jnp.concatenate([mine, from_near[...]], axis=0), weight[...]) + dot(
        jnp.concatenate([mates, from_far[...]], axis=0), mate_weight[...]
    )
    own[...] = both[:rows]
    near[...] = both[rows:].astype(jnp.bfloat16)


def kv_partial(section, hidden, from_near, from_far, weight, mate_weight):
    shape = (hidden.shape[0], weight.shape[1])
    return pl.pallas_call(
        kv_partial_kernel,
        out_shape=(
            jax.ShapeDtypeStruct(shape, jnp.float32),
            jax.ShapeDtypeStruct(shape, jnp.bfloat16),
        ),
        in_specs=[SMEM_SPEC] + [VMEM_SPEC] * 5,
        out_specs=(VMEM_SPEC, VMEM_SPEC),
        compiler_params=pltpu.CompilerParams(vmem_limit_bytes=VMEM_LIMIT),
        name="kv_partial",
    )(section, hidden, from_near, from_far, weight, mate_weight)


def rotate_kernel(signs, own, other, head, tail):
    row = lax.broadcasted_iota(jnp.int32, (HD, HD), 0)
    column = lax.broadcasted_iota(jnp.int32, (HD, HD), 1)
    meet = row & column
    parity = meet ^ (meet >> 4)
    parity = parity ^ (parity >> 2)
    parity = (parity ^ (parity >> 1)) & 1
    table = (1 - 2 * parity).astype(jnp.float32).astype(jnp.bfloat16)
    sign = signs[...].astype(jnp.float32)
    split = head.shape[0]
    for c in range(2):
        columns = slice(c * HD, (c + 1) * HD)
        value = (own[:, columns] + other[:, columns].astype(jnp.float32)) * sign
        top = value.astype(jnp.bfloat16)
        value = value - top.astype(jnp.float32)
        middle = value.astype(jnp.bfloat16)
        low = (value - middle.astype(jnp.float32)).astype(jnp.bfloat16)
        rotated = (dot(low, table) + dot(middle, table)) + dot(top, table)
        rotated = (rotated * jnp.float32(1.0 / math.sqrt(HD))).astype(jnp.bfloat16)
        head[:, columns] = rotated[:split]
        tail[:, columns] = rotated[split:]


def rotate(signs, own, other):
    rows = own.shape[0]
    return pl.pallas_call(
        rotate_kernel,
        out_shape=(
            jax.ShapeDtypeStruct((rows - TAIL, KV), jnp.bfloat16),
            jax.ShapeDtypeStruct((TAIL, KV), jnp.bfloat16),
        ),
        in_specs=[VMEM_SPEC] * 3,
        out_specs=(VMEM_SPEC, VMEM_SPEC),
        name="rotate",
    )(signs, own, other)


def attend_kernel(place, query, body_pos, tail_pos, *refs):
    bodies, tail, out = refs[:-2], refs[-2], refs[-1]
    rows = query.shape[0]
    group = query.shape[1] // HD
    scale = jnp.float32(math.log2(math.e) / math.sqrt(HD))
    section, first = place[0], place[1]
    parts = [(ref, body_pos, section ^ j) for j, ref in enumerate(bodies)]
    parts.append((tail, tail_pos, 0))
    q = jnp.concatenate([query[:, g * HD : (g + 1) * HD] for g in range(group)], axis=0)
    highest = jnp.full((group * rows, 1), -1e30, jnp.float32)
    total = jnp.zeros((group * rows, 2 * HD), jnp.float32)
    for ref, pos, index in parts:
        size = ref.shape[0]
        scores = lax.dot_general(
            q, ref[:, :HD], (((1,), (1,)), ((), ())), preferred_element_type=jnp.float32
        )
        query_pos = first + lax.broadcasted_iota(jnp.int32, (rows, size), 0)
        allowed = pos[pl.ds(index, 1), :] <= query_pos
        scores = jnp.where(allowed[None], scores.reshape(group, rows, size), -jnp.inf)
        scores = scores.reshape(group * rows, size)
        new_high = jnp.maximum(highest, jnp.max(scores, axis=1, keepdims=True))
        weights = jnp.exp2((scores - new_high) * scale).astype(jnp.bfloat16)
        shrink = jnp.exp2((highest - new_high) * scale)
        value = ref[:, HD:]
        value = jnp.concatenate([value, jnp.ones_like(value)], axis=1)
        total = total * shrink + dot(weights, value)
        highest = new_high
    attended = (total[:, :HD] / total[:, HD:]).astype(jnp.bfloat16)
    for g in range(group):
        out[:, g * HD : (g + 1) * HD] = attended[g * rows : (g + 1) * rows]


def attend(place, query, body_pos, tail_pos, bodies, tail):
    return pl.pallas_call(
        attend_kernel,
        out_shape=jax.ShapeDtypeStruct(query.shape, jnp.bfloat16),
        in_specs=[SMEM_SPEC] + [VMEM_SPEC] * (4 + len(bodies)),
        out_specs=VMEM_SPEC,
        compiler_params=pltpu.CompilerParams(vmem_limit_bytes=VMEM_LIMIT),
        name="attend",
    )(place, query, body_pos, tail_pos, *bodies, tail)


def out_kernel(first, weight, out):
    out[0] = dot(first[...], weight[0]).astype(jnp.bfloat16)


def out_project(first, weight, heads):
    sections, depth, width = weight.shape
    each = heads // sections
    share = width // each
    rows = first.shape[0]
    return pl.pallas_call(
        out_kernel,
        grid=(heads,),
        out_shape=jax.ShapeDtypeStruct((heads, rows, share), jnp.bfloat16),
        in_specs=[
            pl.BlockSpec((rows, depth), lambda h: (0, 0)),
            pl.BlockSpec((1, depth, share), lambda h: (h // each, 0, h % each)),
        ],
        out_specs=pl.BlockSpec((1, rows, share), lambda h: (h, 0, 0)),
        name="out_project",
    )(first, weight)


def query_kernel(width, scaled, inverse, weight, out, total, square):
    step = pl.program_id(0)

    @pl.when(step == 0)
    def _():
        total[...] = jnp.zeros_like(total)
        square[...] = jnp.zeros_like(square)

    block = scaled[0]
    total[...] += dot(block, weight[...])
    plain = block.astype(jnp.float32) * inverse[0]
    square[...] += jnp.sum(plain * plain, axis=1, keepdims=True)

    @pl.when(step == pl.num_programs(0) - 1)
    def _():
        root = lax.rsqrt(square[...] / width + 1e-6)
        out[...] = (total[...] * root).astype(jnp.bfloat16)


def query_project(scaled, inverse, weight):
    heads, rows, share = scaled.shape
    width = weight.shape[1]
    return pl.pallas_call(
        functools.partial(query_kernel, heads * share),
        grid=(heads,),
        out_shape=jax.ShapeDtypeStruct((rows, width), jnp.bfloat16),
        in_specs=[
            pl.BlockSpec((1, rows, share), lambda h: (h, 0, 0)),
            pl.BlockSpec((1, 1, share), lambda h: (h, 0, 0)),
            pl.BlockSpec((share, width), lambda h: (h, 0)),
        ],
        out_specs=pl.BlockSpec((rows, width), lambda h: (0, 0)),
        scratch_shapes=[
            pltpu.VMEM((rows, width), jnp.float32),
            pltpu.VMEM((rows, 1), jnp.float32),
        ],
        name="query_project",
    )(scaled, inverse, weight)


def per_device(
    self_hidden, kv_weight, signs, positions, queries, out_weight, query_weight, norm_gain
):
    rows, width = self_hidden.shape
    sections, ctxs, heads = (lax.axis_size(a) for a in ("section", "ctx", "head"))
    section, ctx, head = (lax.axis_index(a) for a in ("section", "ctx", "head"))
    share = width // heads
    depth = width // sections

    def swap_core(value):
        return lax.ppermute(value, "section", [(i, i ^ 1) for i in range(sections)])

    def swap_y(value):
        return lax.ppermute(value, "section", [(i, i ^ 2) for i in range(sections)])

    def swap_far_y(value):
        pairs = [
            (s * heads + h, (s ^ 2) * heads + (h ^ 1))
            for s in range(sections)
            for h in range(heads)
        ]
        return lax.ppermute(value, ("section", "head"), pairs)

    out_all = lax.all_gather(out_weight, "section", axis=0)
    query_all = lax.all_gather(query_weight, "section", axis=0, tiled=True)

    body = rows - TAIL
    pos = positions.reshape(sections, ctxs, rows)
    body_pos = pos[:, :, :body].reshape(sections, ctxs * body)
    tail_pos = jnp.transpose(pos[:, :, body:], (1, 0, 2)).reshape(1, ctxs * sections * TAIL)
    first_pos = lax.dynamic_index_in_dim(positions, (section * ctxs + ctx) * rows, 0, False)
    place = jnp.stack([section, first_pos])

    def columns(of):
        return lax.dynamic_slice_in_dim(self_hidden, of * depth, depth, 1)

    from_near = swap_y(columns(section ^ 2))
    from_far = swap_far_y(columns(section ^ 3))
    mate_weight = swap_core(kv_weight)
    own, near = kv_partial(place, self_hidden, from_near, from_far, kv_weight, mate_weight)
    cache_body, cache_tail = rotate(signs, own, swap_y(near))

    cache_tail = lax.all_gather(cache_tail, "section", axis=0, tiled=True)
    body_own = lax.all_gather(cache_body, "ctx", axis=0, tiled=True)
    body_near = swap_y(body_own)
    body_mate = swap_core(body_own)
    tail = lax.all_gather(cache_tail, "ctx", axis=0, tiled=True)
    body_last = swap_core(body_near)
    bodies = (body_own, body_mate, body_near, body_last)

    first = attend(place, queries, body_pos, tail_pos, bodies, tail)
    partial = out_project(first, out_all, heads)
    pieces = lax.all_to_all(partial, "head", 0, 0, tiled=True)
    own_hidden = lax.dynamic_slice_in_dim(self_hidden, head * share, share, 1)
    residual = own_hidden.astype(jnp.float32) + jnp.sum(pieces.astype(jnp.float32), axis=0)
    gain = norm_gain.astype(jnp.float32)
    own_gain = lax.dynamic_slice_in_dim(gain, head * share, share, 0)
    scaled = (residual * own_gain).astype(jnp.bfloat16)
    spread = jnp.broadcast_to(scaled[None], (heads, rows, share))
    scaled_all = lax.all_to_all(spread, "head", 0, 0, tiled=True)
    inverse = (1.0 / gain).reshape(heads, 1, share)
    second_queries = query_project(scaled_all, inverse, query_all)
    second = attend(place, second_queries, body_pos, tail_pos, bodies, tail)
    return (residual.astype(jnp.bfloat16), second)


def solution(mesh):
    return jax.shard_map(
        per_device,
        mesh=mesh,
        in_specs=(
            P(("section", "ctx"), None),
            P("section", "head"),
            P("head", None),
            P(),
            P(("section", "ctx"), "head"),
            P("head", "section"),
            P("section", "head"),
            P(),
        ),
        out_specs=(P(("section", "ctx"), "head"), P(("section", "ctx"), "head")),
        check_vma=False,
    )
```

```python
import math

import jax
import jax.numpy as jnp
from jax import lax
from jax.experimental import pallas as pl
from jax.experimental.pallas import tpu as pltpu
from jax.sharding import PartitionSpec as P

HD = 128
KV = 2 * HD
SCALE_ROWS = 16
TOP = 13.0
SCORE_SCALE = math.log2(math.e) / math.sqrt(HD)
LIMITS = pltpu.CompilerParams(vmem_limit_bytes=48 * 2**20)

SMEM_SPEC = pl.BlockSpec(memory_space=pltpu.SMEM)
VMEM_SPEC = pl.BlockSpec(memory_space=pltpu.VMEM)


def dot(a, b):
    return jnp.dot(a, b, preferred_element_type=jnp.float32)


def kv_partial_kernel(place, hidden, from_near, from_far, weight, mate_weight, out, send):
    depth = weight.shape[0]
    section = place[0]
    mine = hidden[:, pl.ds(pl.multiple_of(section * depth, depth), depth)]
    mates = hidden[:, pl.ds(pl.multiple_of((section ^ 1) * depth, depth), depth)]
    both = dot(jnp.concatenate([mine, from_near[...]], axis=0), weight[...]) + dot(
        jnp.concatenate([mates, from_far[...]], axis=0), mate_weight[...]
    )
    out[...] = both
    send[...] = both.astype(jnp.bfloat16)


def kv_partial(place, hidden, from_near, from_far, weight, mate_weight):
    shape = (2 * hidden.shape[0], weight.shape[1])
    return pl.pallas_call(
        kv_partial_kernel,
        out_shape=(
            jax.ShapeDtypeStruct(shape, jnp.float32),
            jax.ShapeDtypeStruct(shape, jnp.bfloat16),
        ),
        in_specs=[SMEM_SPEC] + [VMEM_SPEC] * 5,
        out_specs=(VMEM_SPEC, VMEM_SPEC),
        compiler_params=LIMITS,
        name="kv_partial",
    )(place, hidden, from_near, from_far, weight, mate_weight)


def rotate_kernel(place, signs, own, other, out):
    row = lax.broadcasted_iota(jnp.int32, (HD, HD), 0)
    column = lax.broadcasted_iota(jnp.int32, (HD, HD), 1)
    meet = row & column
    parity = meet ^ (meet >> 4)
    parity = parity ^ (parity >> 2)
    parity = (parity ^ (parity >> 1)) & 1
    table = (1 - 2 * parity).astype(jnp.float32).astype(jnp.bfloat16)
    sign = signs[...].astype(jnp.float32)
    rows = own.shape[0] // 2
    side = place[0] >> 1
    for c in range(2):
        columns = slice(c * HD, (c + 1) * HD)
        theirs = other[:, columns].astype(jnp.float32)
        value = own[:, columns] + jnp.concatenate([theirs[rows:], theirs[:rows]], axis=0)
        value = value * sign
        top = value.astype(jnp.bfloat16)
        value = value - top.astype(jnp.float32)
        middle = value.astype(jnp.bfloat16)
        low = (value - middle.astype(jnp.float32)).astype(jnp.bfloat16)
        rotated = (dot(low, table) + dot(middle, table)) + dot(top, table)
        rotated = rotated * jnp.float32(1.0 / math.sqrt(HD))
        rotated = rotated.astype(jnp.bfloat16).astype(jnp.float32)
        peak = jnp.max(jnp.abs(rotated), axis=0, keepdims=True)
        power = jnp.floor(jnp.log2(jnp.maximum(peak, 1e-30)))
        rotated = rotated * jnp.exp2(TOP - power)
        out[pl.ds(pl.multiple_of(side * rows, rows), rows), columns] = rotated[:rows]
        out[pl.ds(pl.multiple_of((1 - side) * rows, rows), rows), columns] = rotated[rows:]
        out[2 * rows :, columns] = jnp.broadcast_to(power, (SCALE_ROWS, HD))


def rotate(place, signs, own, other):
    return pl.pallas_call(
        rotate_kernel,
        out_shape=jax.ShapeDtypeStruct((own.shape[0] + SCALE_ROWS, KV), jnp.float32),
        in_specs=[SMEM_SPEC] + [VMEM_SPEC] * 3,
        out_specs=VMEM_SPEC,
        compiler_params=LIMITS,
        name="rotate",
    )(place, signs, own, other)


def stack_heads(query):
    group = query.shape[1] // HD
    return jnp.concatenate([query[:, g * HD : (g + 1) * HD] for g in range(group)], axis=0)


def absorb(state, q, cache, pos, index, first, rows):
    highest, total = state
    group = q.shape[0] // rows
    size = pos.shape[1]
    for step in range(cache.shape[0] // size):
        keys = cache[step * size : (step + 1) * size, :HD]
        value = cache[step * size : (step + 1) * size, HD:]
        scores = lax.dot_general(
            q, keys, (((1,), (1,)), ((), ())), preferred_element_type=jnp.float32
        )
        query_pos = first + lax.broadcasted_iota(jnp.int32, (rows, size), 0)
        allowed = pos[pl.ds(2 * index + step, 1), :] <= query_pos
        scores = jnp.where(allowed[None], scores.reshape(group, rows, size), -jnp.inf)
        scores = scores.reshape(group * rows, size)
        new_high = jnp.maximum(highest, jnp.max(scores, axis=1, keepdims=True))
        weights = jnp.exp2((scores - new_high) * SCORE_SCALE).astype(jnp.bfloat16)
        shrink = jnp.exp2((highest - new_high) * SCORE_SCALE)
        value = jnp.concatenate([value, jnp.ones_like(value)], axis=1)
        total = total * shrink + dot(weights, value)
        highest = new_high
    return highest, total


def fresh(q):
    return (
        jnp.full((q.shape[0], 1), -1e30, jnp.float32),
        jnp.zeros((q.shape[0], KV), jnp.float32),
    )


def finish(state):
    total = state[1]
    return (total[:, :HD] / total[:, HD:]).astype(jnp.bfloat16)


def own_keys_kernel(place, query, pos, own, high_out, total_out):
    q = stack_heads(query)
    core = place[0] & 1
    highest, total = absorb(fresh(q), q, own, pos, core, place[1], query.shape[0])
    high_out[...] = jnp.broadcast_to(highest, high_out.shape)
    total_out[...] = total


def own_keys(place, query, pos, own):
    stacked = query.shape[0] * query.shape[1] // HD
    return pl.pallas_call(
        own_keys_kernel,
        out_shape=(
            jax.ShapeDtypeStruct((stacked, HD), jnp.float32),
            jax.ShapeDtypeStruct((stacked, KV), jnp.float32),
        ),
        in_specs=[SMEM_SPEC] + [VMEM_SPEC] * 3,
        out_specs=(VMEM_SPEC, VMEM_SPEC),
        compiler_params=LIMITS,
        name="own_keys",
    )(place, query, pos, own)


def first_layer_kernel(place, query, pos, mate, high_in, total_in, weight, out):
    q = stack_heads(query)
    rows = query.shape[0]
    core = place[0] & 1
    state = (high_in[:, :1], total_in[...])
    attended = finish(absorb(state, q, mate, pos, 1 - core, place[1], rows))
    first = jnp.concatenate(
        [attended[g : g + rows] for g in range(0, attended.shape[0], rows)], axis=1
    )
    sections, share = weight.shape[0], out.shape[2]
    each = out.shape[0] // sections
    for h in range(out.shape[0]):
        columns = slice((h % each) * share, (h % each + 1) * share)
        out[h] = dot(first, weight[h // each, :, columns]).astype(jnp.bfloat16)


def first_layer(place, query, pos, mate, state, weight, heads):
    rows = query.shape[0]
    share = weight.shape[0] * weight.shape[2] // heads
    return pl.pallas_call(
        first_layer_kernel,
        out_shape=jax.ShapeDtypeStruct((heads, rows, share), jnp.bfloat16),
        in_specs=[SMEM_SPEC] + [VMEM_SPEC] * 6,
        out_specs=VMEM_SPEC,
        compiler_params=LIMITS,
        name="first_layer",
    )(place, query, pos, mate, *state, weight)


def residual_kernel(pieces, hidden, gain, stream, spread):
    total = hidden[...].astype(jnp.float32)
    for h in range(pieces.shape[0]):
        total = total + pieces[h].astype(jnp.float32)
    stream[...] = total.astype(jnp.bfloat16)
    scaled = (total * gain[...]).astype(jnp.bfloat16)
    for h in range(pieces.shape[0]):
        spread[h] = scaled


def residual_sum(pieces, hidden, gain):
    return pl.pallas_call(
        residual_kernel,
        out_shape=(
            jax.ShapeDtypeStruct(hidden.shape, jnp.bfloat16),
            jax.ShapeDtypeStruct(pieces.shape, jnp.bfloat16),
        ),
        in_specs=[VMEM_SPEC] * 3,
        out_specs=(VMEM_SPEC, VMEM_SPEC),
        compiler_params=LIMITS,
        name="residual_sum",
    )(pieces, hidden, gain)


def second_layer_kernel(place, scaled, inverse, weight, pos, own, mate, out):
    heads, rows, share = scaled.shape
    total = jnp.zeros((rows, weight.shape[1]), jnp.float32)
    square = jnp.zeros((rows, 1), jnp.float32)
    for h in range(heads):
        block = scaled[h]
        total = total + dot(block, weight[h * share : (h + 1) * share])
        plain = block.astype(jnp.float32) * inverse[h : h + 1]
        square = square + jnp.sum(plain * plain, axis=1, keepdims=True)
    root = lax.rsqrt(square / (heads * share) + 1e-6)
    q = stack_heads((total * root).astype(jnp.bfloat16))
    core = place[0] & 1
    state = absorb(fresh(q), q, own, pos, core, place[1], rows)
    attended = finish(absorb(state, q, mate, pos, 1 - core, place[1], rows))
    for g in range(out.shape[1] // HD):
        out[:, g * HD : (g + 1) * HD] = attended[g * rows : (g + 1) * rows]


def second_layer(place, scaled, inverse, weight, pos, own, mate):
    return pl.pallas_call(
        second_layer_kernel,
        out_shape=jax.ShapeDtypeStruct((scaled.shape[1], weight.shape[1]), jnp.bfloat16),
        in_specs=[SMEM_SPEC] + [VMEM_SPEC] * 6,
        out_specs=VMEM_SPEC,
        compiler_params=LIMITS,
        name="second_layer",
    )(place, scaled, inverse, weight, pos, own, mate)


def per_device(
    self_hidden, kv_weight, signs, positions, queries, out_weight, query_weight, norm_gain
):
    rows, width = self_hidden.shape
    sections, ctxs, heads = (lax.axis_size(a) for a in ("section", "ctx", "head"))
    section, ctx, head = (lax.axis_index(a) for a in ("section", "ctx", "head"))
    share = width // heads
    depth = width // sections

    def swap_core(value):
        return lax.ppermute(value, "section", [(i, i ^ 1) for i in range(sections)])

    def swap_y(value):
        return lax.ppermute(value, "section", [(i, i ^ 2) for i in range(sections)])

    def swap_far_y(value):
        pairs = [
            (s * heads + h, (s ^ 2) * heads + (h ^ 1))
            for s in range(sections)
            for h in range(heads)
        ]
        return lax.ppermute(value, ("section", "head"), pairs)

    def columns(of):
        return lax.dynamic_slice_in_dim(self_hidden, of * depth, depth, 1)

    first_pos = lax.dynamic_index_in_dim(positions, (section * ctxs + ctx) * rows, 0, False)
    place = jnp.stack([section, first_pos])
    pos = positions.reshape(2, sections // 2, ctxs, rows)
    pos = jnp.transpose(pos, (1, 2, 0, 3)).reshape(sections, ctxs * rows)

    from_near = swap_y(columns(section ^ 2))
    from_far = swap_far_y(columns(section ^ 3))
    mate_weight = swap_core(kv_weight)

    out_all = lax.all_gather(out_weight, "section", axis=0)
    query_all = lax.all_gather(query_weight, "section", axis=0, tiled=True)

    own, send = kv_partial(place, self_hidden, from_near, from_far, kv_weight, mate_weight)
    coded = rotate(place, signs, own, swap_y(send)).astype(jnp.float16)
    coded = lax.all_gather(coded, "ctx", axis=0).astype(jnp.float32)
    power = coded[:, 2 * rows : 2 * rows + 1]
    cache_own = (coded[:, : 2 * rows] * jnp.exp2(power - TOP)).astype(jnp.bfloat16)
    cache_own = cache_own.reshape(ctxs * 2 * rows, KV)
    cache_mate = swap_core(cache_own)

    state = own_keys(place, queries, pos, cache_own)
    partial = first_layer(place, queries, pos, cache_mate, state, out_all, heads)
    pieces = lax.all_to_all(partial, "head", 0, 0, tiled=True)
    own_hidden = lax.dynamic_slice_in_dim(self_hidden, head * share, share, 1)
    gain = norm_gain.astype(jnp.float32)
    own_gain = lax.dynamic_slice_in_dim(gain, head * share, share, 0)
    stream, spread = residual_sum(pieces, own_hidden, own_gain.reshape(1, share))
    scaled_all = lax.all_to_all(spread, "head", 0, 0, tiled=True)
    inverse = (1.0 / gain).reshape(heads, share)
    second = second_layer(place, scaled_all, inverse, query_all, pos, cache_own, cache_mate)
    return (stream, second)


def solution(mesh):
    return jax.shard_map(
        per_device,
        mesh=mesh,
        in_specs=(
            P(("section", "ctx"), None),
            P("section", "head"),
            P("head", None),
            P(),
            P(("section", "ctx"), "head"),
            P("head", "section"),
            P("section", "head"),
            P(),
        ),
        out_specs=(P(("section", "ctx"), "head"), P(("section", "ctx"), "head")),
        check_vma=False,
    )
```

```python
import math

import jax
import jax.numpy as jnp
from jax import lax
from jax.experimental import pallas as pl
from jax.experimental.pallas import tpu as pltpu
from jax.sharding import PartitionSpec as P

HD = 128
KV = 2 * HD
SCALE_ROWS = 16
TOP = 13.0
SCORE_SCALE = math.log2(math.e) / math.sqrt(HD)


def limit(mebibytes):
    return pltpu.CompilerParams(vmem_limit_bytes=mebibytes * 2**20)


SMEM_SPEC = pl.BlockSpec(memory_space=pltpu.SMEM)
VMEM_SPEC = pl.BlockSpec(memory_space=pltpu.VMEM)
HBM_SPEC = pl.BlockSpec(memory_space=pltpu.HBM)


def in_hbm(value):
    return pltpu.with_memory_space_constraint(value, pltpu.HBM)


def dot(a, b):
    return jnp.dot(a, b, preferred_element_type=jnp.float32)


def kv_own_kernel(place, hidden, weight, mate_weight, out):
    depth = weight.shape[0]
    section = place[0]
    mine = hidden[:, pl.ds(pl.multiple_of(section * depth, depth), depth)]
    mates = hidden[:, pl.ds(pl.multiple_of((section ^ 1) * depth, depth), depth)]
    out[...] = dot(mine, weight[...]) + dot(mates, mate_weight[...])


def kv_own(place, hidden, weight, mate_weight):
    return pl.pallas_call(
        kv_own_kernel,
        out_shape=jax.ShapeDtypeStruct((hidden.shape[0], weight.shape[1]), jnp.float32),
        in_specs=[SMEM_SPEC] + [VMEM_SPEC] * 3,
        out_specs=VMEM_SPEC,
        compiler_params=limit(16),
        name="kv_own",
    )(place, hidden, weight, mate_weight)


def kv_near_kernel(own, from_near, from_far, weight, mate_weight, out, send):
    rows = own.shape[0]
    near = dot(from_near[...], weight[...]) + dot(from_far[...], mate_weight[...])
    out[:rows] = own[...]
    out[rows:] = near
    send[:rows] = own[...].astype(jnp.bfloat16)
    send[rows:] = near.astype(jnp.bfloat16)


def kv_near(own, from_near, from_far, weight, mate_weight):
    shape = (2 * own.shape[0], own.shape[1])
    return pl.pallas_call(
        kv_near_kernel,
        out_shape=(
            jax.ShapeDtypeStruct(shape, jnp.float32),
            jax.ShapeDtypeStruct(shape, jnp.bfloat16),
        ),
        in_specs=[VMEM_SPEC] * 5,
        out_specs=(VMEM_SPEC, VMEM_SPEC),
        compiler_params=limit(16),
        name="kv_near",
    )(own, from_near, from_far, weight, mate_weight)


def rotate_kernel(place, signs, own, other, out):
    row = lax.broadcasted_iota(jnp.int32, (HD, HD), 0)
    column = lax.broadcasted_iota(jnp.int32, (HD, HD), 1)
    meet = row & column
    parity = meet ^ (meet >> 4)
    parity = parity ^ (parity >> 2)
    parity = (parity ^ (parity >> 1)) & 1
    table = (1 - 2 * parity).astype(jnp.float32).astype(jnp.bfloat16)
    sign = signs[...].astype(jnp.float32)
    rows = own.shape[0] // 2
    side = place[0] >> 1
    for c in range(2):
        columns = slice(c * HD, (c + 1) * HD)
        theirs = other[:, columns].astype(jnp.float32)
        value = own[:, columns] + jnp.concatenate([theirs[rows:], theirs[:rows]], axis=0)
        value = value * sign
        top = value.astype(jnp.bfloat16)
        value = value - top.astype(jnp.float32)
        middle = value.astype(jnp.bfloat16)
        low = (value - middle.astype(jnp.float32)).astype(jnp.bfloat16)
        rotated = (dot(low, table) + dot(middle, table)) + dot(top, table)
        rotated = rotated * jnp.float32(1.0 / math.sqrt(HD))
        rotated = rotated.astype(jnp.bfloat16).astype(jnp.float32)
        peak = jnp.max(jnp.abs(rotated), axis=0, keepdims=True)
        power = jnp.floor(jnp.log2(jnp.maximum(peak, 1e-30)))
        rotated = rotated * jnp.exp2(TOP - power)
        out[pl.ds(pl.multiple_of(side * rows, rows), rows), columns] = rotated[:rows]
        out[pl.ds(pl.multiple_of((1 - side) * rows, rows), rows), columns] = rotated[rows:]
        out[2 * rows :, columns] = jnp.broadcast_to(power, (SCALE_ROWS, HD))


def rotate(place, signs, own, other):
    return pl.pallas_call(
        rotate_kernel,
        out_shape=jax.ShapeDtypeStruct((own.shape[0] + SCALE_ROWS, KV), jnp.float32),
        in_specs=[SMEM_SPEC] + [VMEM_SPEC] * 3,
        out_specs=VMEM_SPEC,
        compiler_params=limit(16),
        name="rotate",
    )(place, signs, own, other)


def stack_heads(query):
    group = query.shape[1] // HD
    return jnp.concatenate([query[:, g * HD : (g + 1) * HD] for g in range(group)], axis=0)


def absorb(state, q, cache, pos, index, first, rows, loads=()):
    highest, total = state
    group = q.shape[0] // rows
    size = pos.shape[1]
    for step in range(cache.shape[0] // size):
        if loads:
            loads[step].wait()
        keys = cache[step * size : (step + 1) * size, :HD]
        value = cache[step * size : (step + 1) * size, HD:]
        scores = lax.dot_general(
            q, keys, (((1,), (1,)), ((), ())), preferred_element_type=jnp.float32
        )
        query_pos = first + lax.broadcasted_iota(jnp.int32, (rows, size), 0)
        allowed = pos[pl.ds(2 * index + step, 1), :] <= query_pos
        scores = jnp.where(allowed[None], scores.reshape(group, rows, size), -jnp.inf)
        scores = scores.reshape(group * rows, size)
        new_high = jnp.maximum(highest, jnp.max(scores, axis=1, keepdims=True))
        weights = jnp.exp2((scores - new_high) * SCORE_SCALE).astype(jnp.bfloat16)
        shrink = jnp.exp2((highest - new_high) * SCORE_SCALE)
        value = jnp.concatenate([value, jnp.ones_like(value)], axis=1)
        total = total * shrink + dot(weights, value)
        highest = new_high
    return highest, total


def load_rows(source, target, sem, parts):
    size = source.shape[0] // parts
    copies = []
    for i in range(parts):
        rows = pl.ds(i * size, size)
        copies.append(pltpu.make_async_copy(source.at[rows], target.at[rows], sem.at[i]))
        copies[-1].start()
    return copies


def fresh(q):
    return (
        jnp.full((q.shape[0], 1), -1e30, jnp.float32),
        jnp.zeros((q.shape[0], KV), jnp.float32),
    )


def finish(state):
    total = state[1]
    return (total[:, :HD] / total[:, HD:]).astype(jnp.bfloat16)


def own_keys_kernel(place, query, pos, own, high_out, total_out):
    q = stack_heads(query)
    core = place[0] & 1
    highest, total = absorb(fresh(q), q, own, pos, core, place[1], query.shape[0])
    high_out[...] = jnp.broadcast_to(highest, high_out.shape)
    total_out[...] = total


def own_keys(place, query, pos, own):
    stacked = query.shape[0] * query.shape[1] // HD
    return pl.pallas_call(
        own_keys_kernel,
        out_shape=(
            pltpu.VMEM((stacked, HD), jnp.float32),
            pltpu.VMEM((stacked, KV), jnp.float32),
        ),
        in_specs=[SMEM_SPEC] + [VMEM_SPEC] * 3,
        out_specs=(VMEM_SPEC, VMEM_SPEC),
        compiler_params=limit(24),
        name="own_keys",
    )(place, query, pos, own)


def first_layer_kernel(
    place, query, pos, high_in, total_in, mate, weight, out, near, held, stage, mate_sem, sem, out_sem
):
    sections = weight.shape[0]
    mate_loads = load_rows(mate, near, mate_sem, mate.shape[0] // pos.shape[1])
    loads = load_rows(weight, held, sem, sections)
    q = stack_heads(query)
    rows = query.shape[0]
    core = place[0] & 1
    state = (high_in[:, :1], total_in[...])
    state = absorb(state, q, near, pos, 1 - core, place[1], rows, mate_loads)
    attended = finish(state)
    first = jnp.concatenate(
        [attended[g : g + rows] for g in range(0, attended.shape[0], rows)], axis=1
    )
    heads, _, share = stage.shape
    each = heads // sections
    stores = []
    for h in range(heads):
        if h % each == 0:
            loads[h // each].wait()
        columns = slice((h % each) * share, (h % each + 1) * share)
        stage[h] = dot(first, held[h // each, :, columns]).astype(jnp.bfloat16)
        stores.append(pltpu.make_async_copy(stage.at[h], out.at[h], out_sem.at[h]))
        stores[-1].start()
    for store in stores:
        store.wait()


def first_layer(place, query, pos, state, mate, weight, heads):
    rows = query.shape[0]
    sections, _, width = weight.shape
    shape = (heads, rows, sections * width // heads)
    return pl.pallas_call(
        first_layer_kernel,
        out_shape=pltpu.HBM(shape, jnp.bfloat16),
        in_specs=[SMEM_SPEC] + [VMEM_SPEC] * 4 + [HBM_SPEC] * 2,
        out_specs=HBM_SPEC,
        scratch_shapes=[
            pltpu.VMEM(mate.shape, jnp.bfloat16),
            pltpu.VMEM(weight.shape, jnp.bfloat16),
            pltpu.VMEM(shape, jnp.bfloat16),
            pltpu.SemaphoreType.DMA((mate.shape[0] // pos.shape[1],)),
            pltpu.SemaphoreType.DMA((sections,)),
            pltpu.SemaphoreType.DMA((heads,)),
        ],
        compiler_params=limit(32),
        name="first_layer",
    )(place, query, pos, *state, in_hbm(mate), in_hbm(weight))


def residual_kernel(pieces, hidden, gain, stream, spread, scaled, sem):
    total = hidden[...].astype(jnp.float32)
    for h in range(pieces.shape[0]):
        total = total + pieces[h].astype(jnp.float32)
    scaled[...] = (total * gain[...]).astype(jnp.bfloat16)
    stores = [
        pltpu.make_async_copy(scaled, spread.at[h], sem.at[h]) for h in range(spread.shape[0])
    ]
    for store in stores:
        store.start()
    stream[...] = total.astype(jnp.bfloat16)
    for store in stores:
        store.wait()


def residual_sum(pieces, hidden, gain):
    return pl.pallas_call(
        residual_kernel,
        out_shape=(
            jax.ShapeDtypeStruct(hidden.shape, jnp.bfloat16),
            pltpu.HBM(pieces.shape, jnp.bfloat16),
        ),
        in_specs=[VMEM_SPEC] * 3,
        out_specs=(VMEM_SPEC, HBM_SPEC),
        scratch_shapes=[
            pltpu.VMEM(hidden.shape, jnp.bfloat16),
            pltpu.SemaphoreType.DMA((pieces.shape[0],)),
        ],
        compiler_params=limit(16),
        name="residual_sum",
    )(pieces, hidden, gain)


def second_layer_kernel(
    place, scaled, inverse, pos, own, near, far, mate, out, held, other, sem, mate_sem
):
    heads, rows, share = scaled.shape
    half = heads // 2
    each = half // near.shape[0]
    core, side = place[0] & 1, place[0] >> 1
    loads = [
        load_rows(weight, held.at[i], sem.at[i], weight.shape[0])
        for i, weight in enumerate((near, far))
    ]
    mate_loads = load_rows(mate, other, mate_sem, mate.shape[0] // pos.shape[1])
    square = jnp.zeros((rows, 1), jnp.float32)
    for h in range(heads):
        plain = scaled[h].astype(jnp.float32) * inverse[h : h + 1]
        square = square + jnp.sum(plain * plain, axis=1, keepdims=True)
    root = lax.rsqrt(square / (heads * share) + 1e-6)
    total = jnp.zeros((rows, near.shape[2]), jnp.float32)
    for i in range(2):
        for k in range(half):
            if k % each == 0:
                loads[i][k // each].wait()
            part = held[i, k // each, (k % each) * share : (k % each + 1) * share]
            total = total + dot(scaled[(side ^ i) * half + k], part)
    q = stack_heads((total * root).astype(jnp.bfloat16))
    state = absorb(fresh(q), q, own, pos, core, place[1], rows)
    state = absorb(state, q, other, pos, 1 - core, place[1], rows, mate_loads)
    attended = finish(state)
    for g in range(out.shape[1] // HD):
        out[:, g * HD : (g + 1) * HD] = attended[g * rows : (g + 1) * rows]


def second_layer(place, scaled, inverse, pos, own, near, far, mate):
    parts = mate.shape[0] // pos.shape[1]
    return pl.pallas_call(
        second_layer_kernel,
        out_shape=jax.ShapeDtypeStruct((scaled.shape[1], near.shape[2]), jnp.bfloat16),
        in_specs=[SMEM_SPEC] + [VMEM_SPEC] * 4 + [HBM_SPEC] * 3,
        out_specs=VMEM_SPEC,
        scratch_shapes=[
            pltpu.VMEM((2,) + near.shape, jnp.bfloat16),
            pltpu.VMEM(mate.shape, jnp.bfloat16),
            pltpu.SemaphoreType.DMA((2, near.shape[0])),
            pltpu.SemaphoreType.DMA((parts,)),
        ],
        compiler_params=limit(36),
        name="second_layer",
    )(place, scaled, inverse, pos, own, in_hbm(near), in_hbm(far), in_hbm(mate))


def per_device(
    self_hidden, kv_weight, signs, positions, queries, out_weight, query_weight, norm_gain
):
    rows, width = self_hidden.shape
    sections, ctxs, heads = (lax.axis_size(a) for a in ("section", "ctx", "head"))
    section, ctx, head = (lax.axis_index(a) for a in ("section", "ctx", "head"))
    share = width // heads
    depth = width // sections

    def swap_core(value):
        return lax.ppermute(value, "section", [(i, i ^ 1) for i in range(sections)])

    def swap_y(value):
        return lax.ppermute(value, "section", [(i, i ^ 2) for i in range(sections)])

    def swap_far_y(value):
        pairs = [
            (s * heads + h, (s ^ 2) * heads + (h ^ 1))
            for s in range(sections)
            for h in range(heads)
        ]
        return lax.ppermute(value, ("section", "head"), pairs)

    def columns(of):
        return lax.dynamic_slice_in_dim(self_hidden, of * depth, depth, 1)

    here = section.reshape(1)
    first_pos = lax.dynamic_index_in_dim(positions, (section * ctxs + ctx) * rows, 0, False)
    place = jnp.stack([section, first_pos])
    pos = positions.reshape(2, sections // 2, ctxs, rows)
    pos = jnp.transpose(pos, (1, 2, 0, 3)).reshape(sections, ctxs * rows)

    def pair(value):
        groups = [[i, i + 1] for i in range(0, sections, 2)]
        return lax.all_gather(value, "section", axis=0, axis_index_groups=groups)

    near_columns = columns(section ^ 2)
    far_columns = columns(section ^ 3)
    from_near = swap_y(near_columns)
    from_far = swap_far_y(far_columns)
    near_columns, far_columns, moved_weight = lax.optimization_barrier(
        (near_columns, far_columns, kv_weight)
    )
    mate_weight = swap_core(moved_weight)
    own_hidden = lax.dynamic_slice_in_dim(self_hidden, head * share, share, 1)
    mate_weight, own_hidden = lax.optimization_barrier((mate_weight, own_hidden))
    own = kv_own(here, self_hidden, kv_weight, mate_weight)
    own, send = kv_near(own, from_near, from_far, kv_weight, mate_weight)
    other = swap_y(send)
    out_all = lax.all_gather(out_weight, "section", axis=0)
    query_near = pair(query_weight)
    send, moved_query = lax.optimization_barrier((send, query_weight))
    query_far = swap_y(moved_query)
    gain = norm_gain.astype(jnp.float32)
    own_gain = lax.dynamic_slice_in_dim(gain, head * share, share, 0).reshape(1, share)
    inverse = (1.0 / gain).reshape(heads, share)
    other, place, pos, own_gain, inverse = lax.optimization_barrier(
        (other, place, pos, own_gain, inverse)
    )
    turned = rotate(here, signs, own, other).astype(jnp.float16)
    coded = lax.all_gather(turned, "ctx", axis=0)
    coded, query_far = lax.optimization_barrier((coded, query_far))
    coded = coded.astype(jnp.float32)
    power = coded[:, 2 * rows : 2 * rows + 1]
    cache_own = (coded[:, : 2 * rows] * jnp.exp2(power - TOP)).astype(jnp.bfloat16)
    cache_own = cache_own.reshape(ctxs * 2 * rows, KV)
    cache_mate = swap_core(cache_own)
    state = own_keys(place, queries, pos, cache_own)
    partial = first_layer(place, queries, pos, state, cache_mate, out_all, heads)
    pieces = lax.all_to_all(partial, "head", 0, 0, tiled=True)
    pieces, query_far = lax.optimization_barrier((pieces, query_far))
    query_far = pair(query_far)
    stream, spread = residual_sum(pieces, own_hidden, own_gain)
    scaled_all = lax.all_to_all(spread, "head", 0, 0, tiled=True)
    second = second_layer(
        place, scaled_all, inverse, pos, cache_own, query_near, query_far, cache_mate
    )
    return (stream, second)


def solution(mesh):
    return jax.shard_map(
        per_device,
        mesh=mesh,
        in_specs=(
            P(("section", "ctx"), None),
            P("section", "head"),
            P("head", None),
            P(),
            P(("section", "ctx"), "head"),
            P("head", "section"),
            P("section", "head"),
            P(),
        ),
        out_specs=(P(("section", "ctx"), "head"), P(("section", "ctx"), "head")),
        check_vma=False,
    )
```

```python
import functools
import math

import jax
import jax.numpy as jnp
from jax import lax
from jax.experimental import pallas as pl
from jax.experimental.pallas import tpu as pltpu
from jax.sharding import PartitionSpec as P

HD = 128
KV = 2 * HD
SCALE_ROWS = 16
HALVES = 1
TOP = 13.0
SCORE_SCALE = math.log2(math.e) / math.sqrt(HD)


def limit(mebibytes):
    return pltpu.CompilerParams(vmem_limit_bytes=mebibytes * 2**20)


SMEM_SPEC = pl.BlockSpec(memory_space=pltpu.SMEM)
VMEM_SPEC = pl.BlockSpec(memory_space=pltpu.VMEM)
HBM_SPEC = pl.BlockSpec(memory_space=pltpu.HBM)


def in_vmem(value):
    return pltpu.with_memory_space_constraint(value, pltpu.VMEM)


def in_hbm(value):
    return pltpu.with_memory_space_constraint(value, pltpu.HBM)


def dot(a, b):
    return jnp.dot(a, b, preferred_element_type=jnp.float32)


def kv_own_kernel(place, hidden, weight, mate_weight, out):
    depth = weight.shape[0]
    section = place[0]
    mine = hidden[:, pl.ds(pl.multiple_of(section * depth, depth), depth)]
    mates = hidden[:, pl.ds(pl.multiple_of((section ^ 1) * depth, depth), depth)]
    out[...] = dot(mine, weight[...]) + dot(mates, mate_weight[...])


def kv_own(place, hidden, weight, mate_weight):
    return pl.pallas_call(
        kv_own_kernel,
        out_shape=jax.ShapeDtypeStruct((hidden.shape[0], weight.shape[1]), jnp.float32),
        in_specs=[SMEM_SPEC] + [VMEM_SPEC] * 3,
        out_specs=VMEM_SPEC,
        compiler_params=limit(16),
        name="kv_own",
    )(place, hidden, weight, mate_weight)


def kv_near_kernel(own, from_near, from_far, weight, mate_weight, out, send):
    rows = own.shape[0]
    near = dot(from_near[...], weight[...]) + dot(from_far[...], mate_weight[...])
    out[:rows] = own[...]
    out[rows:] = near
    send[:rows] = own[...].astype(jnp.bfloat16)
    send[rows:] = near.astype(jnp.bfloat16)


def kv_near(own, from_near, from_far, weight, mate_weight):
    shape = (2 * own.shape[0], own.shape[1])
    return pl.pallas_call(
        kv_near_kernel,
        out_shape=(
            jax.ShapeDtypeStruct(shape, jnp.float32),
            jax.ShapeDtypeStruct(shape, jnp.bfloat16),
        ),
        in_specs=[VMEM_SPEC] * 5,
        out_specs=(VMEM_SPEC, VMEM_SPEC),
        compiler_params=limit(16),
        name="kv_near",
    )(own, from_near, from_far, weight, mate_weight)


def rotate_kernel(place, signs, own, other, out):
    row = lax.broadcasted_iota(jnp.int32, (HD, HD), 0)
    column = lax.broadcasted_iota(jnp.int32, (HD, HD), 1)
    meet = row & column
    parity = meet ^ (meet >> 4)
    parity = parity ^ (parity >> 2)
    parity = (parity ^ (parity >> 1)) & 1
    table = (1 - 2 * parity).astype(jnp.float32).astype(jnp.bfloat16)
    sign = signs[...].astype(jnp.float32)
    rows = own.shape[0] // 2
    side = place[0] >> 1
    for c in range(2):
        columns = slice(c * HD, (c + 1) * HD)
        theirs = other[:, columns].astype(jnp.float32)
        value = own[:, columns] + jnp.concatenate([theirs[rows:], theirs[:rows]], axis=0)
        value = value * sign
        top = value.astype(jnp.bfloat16)
        value = value - top.astype(jnp.float32)
        middle = value.astype(jnp.bfloat16)
        low = (value - middle.astype(jnp.float32)).astype(jnp.bfloat16)
        rotated = (dot(low, table) + dot(middle, table)) + dot(top, table)
        rotated = rotated * jnp.float32(1.0 / math.sqrt(HD))
        rotated = rotated.astype(jnp.bfloat16).astype(jnp.float32)
        peak = jnp.max(jnp.abs(rotated), axis=0, keepdims=True)
        power = jnp.floor(jnp.log2(jnp.maximum(peak, 1e-30)))
        rotated = rotated * jnp.exp2(TOP - power)
        out[pl.ds(pl.multiple_of(side * rows, rows), rows), columns] = rotated[:rows]
        out[pl.ds(pl.multiple_of((1 - side) * rows, rows), rows), columns] = rotated[rows:]
        out[2 * rows :, columns] = jnp.broadcast_to(power, (SCALE_ROWS, HD))


def rotate(place, signs, own, other):
    return pl.pallas_call(
        rotate_kernel,
        out_shape=jax.ShapeDtypeStruct((own.shape[0] + SCALE_ROWS, KV), jnp.float32),
        in_specs=[SMEM_SPEC] + [VMEM_SPEC] * 3,
        out_specs=VMEM_SPEC,
        compiler_params=limit(16),
        name="rotate",
    )(place, signs, own, other)


def stack_heads(query):
    group = query.shape[1] // HD
    return jnp.concatenate([query[:, g * HD : (g + 1) * HD] for g in range(group)], axis=0)


def absorb(state, q, cache, pos, index, first, rows):
    highest, total = state
    group = q.shape[0] // rows
    size = pos.shape[1]
    for step in range(cache.shape[0] // size):
        keys = cache[step * size : (step + 1) * size, :HD]
        value = cache[step * size : (step + 1) * size, HD:]
        scores = lax.dot_general(
            q, keys, (((1,), (1,)), ((), ())), preferred_element_type=jnp.float32
        )
        query_pos = first + lax.broadcasted_iota(jnp.int32, (rows, size), 0)
        allowed = pos[pl.ds(2 * index + step, 1), :] <= query_pos
        scores = jnp.where(allowed[None], scores.reshape(group, rows, size), -jnp.inf)
        scores = scores.reshape(group * rows, size)
        new_high = jnp.maximum(highest, jnp.max(scores, axis=1, keepdims=True))
        weights = jnp.exp2((scores - new_high) * SCORE_SCALE).astype(jnp.bfloat16)
        shrink = jnp.exp2((highest - new_high) * SCORE_SCALE)
        value = jnp.concatenate([value, jnp.ones_like(value)], axis=1)
        total = total * shrink + dot(weights, value)
        highest = new_high
    return highest, total


def load_rows(source, target, sem, parts):
    size = source.shape[0] // parts
    copies = []
    for i in range(parts):
        rows = pl.ds(i * size, size)
        copies.append(pltpu.make_async_copy(source.at[rows], target.at[rows], sem.at[i]))
        copies[-1].start()
    return copies


def fresh(q):
    return (
        jnp.full((q.shape[0], 1), -1e30, jnp.float32),
        jnp.zeros((q.shape[0], KV), jnp.float32),
    )


def finish(state):
    total = state[1]
    return (total[:, :HD] / total[:, HD:]).astype(jnp.bfloat16)


def own_keys_kernel(place, query, pos, own, high_out, total_out):
    q = stack_heads(query)
    core = place[0] & 1
    highest, total = absorb(fresh(q), q, own, pos, core, place[1], query.shape[0])
    high_out[...] = jnp.broadcast_to(highest, high_out.shape)
    total_out[...] = total


def own_keys(place, query, pos, own):
    stacked = query.shape[0] * query.shape[1] // HD
    return pl.pallas_call(
        own_keys_kernel,
        out_shape=(
            pltpu.VMEM((stacked, HD), jnp.float32),
            pltpu.VMEM((stacked, KV), jnp.float32),
        ),
        in_specs=[SMEM_SPEC] + [VMEM_SPEC] * 3,
        out_specs=(VMEM_SPEC, VMEM_SPEC),
        compiler_params=limit(24),
        name="own_keys",
    )(place, query, pos, own)


def first_layer_kernel(
    half, place, query, pos, mate, high_in, total_in, weight, out, held, stage, sem, out_sem
):
    sections = weight.shape[0]
    loads = load_rows(weight, held, sem, sections)
    heads, rows, share = stage.shape
    first_row = half * rows

    def mine(value):
        starts = range(first_row, value.shape[0], query.shape[0])
        return jnp.concatenate([value[i : i + rows] for i in starts], axis=0)

    q = stack_heads(query[first_row : first_row + rows])
    core = place[0] & 1
    state = (mine(high_in)[:, :1], mine(total_in))
    attended = finish(absorb(state, q, mate, pos, 1 - core, place[1] + first_row, rows))
    first = jnp.concatenate(
        [attended[g : g + rows] for g in range(0, attended.shape[0], rows)], axis=1
    )
    each = heads // sections
    stores = []
    for h in range(heads):
        if h % each == 0:
            loads[h // each].wait()
        columns = slice((h % each) * share, (h % each + 1) * share)
        stage[h] = dot(first, held[h // each, :, columns]).astype(jnp.bfloat16)
        stores.append(pltpu.make_async_copy(stage.at[h], out.at[h], out_sem.at[h]))
        stores[-1].start()
    for store in stores:
        store.wait()


def first_layer(half, place, query, pos, mate, state, weight, heads):
    rows = query.shape[0] // HALVES
    sections, _, width = weight.shape
    shape = (heads, rows, sections * width // heads)
    return pl.pallas_call(
        functools.partial(first_layer_kernel, half),
        out_shape=pltpu.HBM(shape, jnp.bfloat16),
        in_specs=[SMEM_SPEC] + [VMEM_SPEC] * 5 + [HBM_SPEC],
        out_specs=HBM_SPEC,
        scratch_shapes=[
            pltpu.VMEM(weight.shape, jnp.bfloat16),
            pltpu.VMEM(shape, jnp.bfloat16),
            pltpu.SemaphoreType.DMA((sections,)),
            pltpu.SemaphoreType.DMA((heads,)),
        ],
        compiler_params=limit(28),
        name="first_layer",
    )(place, query, pos, in_vmem(mate), *state, in_hbm(weight))


def residual_kernel(pieces, hidden, gain, stream, spread, scaled, sem):
    total = hidden[...].astype(jnp.float32)
    for h in range(pieces.shape[0]):
        total = total + pieces[h].astype(jnp.float32)
    scaled[...] = (total * gain[...]).astype(jnp.bfloat16)
    stores = [
        pltpu.make_async_copy(scaled, spread.at[h], sem.at[h]) for h in range(spread.shape[0])
    ]
    for store in stores:
        store.start()
    stream[...] = total.astype(jnp.bfloat16)
    for store in stores:
        store.wait()


def residual_sum(pieces, hidden, gain):
    return pl.pallas_call(
        residual_kernel,
        out_shape=(
            jax.ShapeDtypeStruct(hidden.shape, jnp.bfloat16),
            pltpu.HBM(pieces.shape, jnp.bfloat16),
        ),
        in_specs=[VMEM_SPEC] * 3,
        out_specs=(VMEM_SPEC, HBM_SPEC),
        scratch_shapes=[
            pltpu.VMEM(hidden.shape, jnp.bfloat16),
            pltpu.SemaphoreType.DMA((pieces.shape[0],)),
        ],
        compiler_params=limit(16),
        name="residual_sum",
    )(pieces, hidden, gain)


def second_layer_kernel(
    half, place, scaled, inverse, pos, own, mate, near, far, out
):
    heads, rows, share = scaled.shape
    group = heads // 2
    each = group // near.shape[0]
    core, side = place[0] & 1, place[0] >> 1
    square = jnp.zeros((rows, 1), jnp.float32)
    for h in range(heads):
        plain = scaled[h].astype(jnp.float32) * inverse[h : h + 1]
        square = square + jnp.sum(plain * plain, axis=1, keepdims=True)
    root = lax.rsqrt(square / (heads * share) + 1e-6)
    total = jnp.zeros((rows, near.shape[2]), jnp.float32)
    for i, weight in enumerate((near, far)):
        for k in range(group):
            part = weight[k // each, (k % each) * share : (k % each + 1) * share]
            total = total + dot(scaled[(side ^ i) * group + k], part)
    q = stack_heads((total * root).astype(jnp.bfloat16))
    first_pos = place[1] + half * rows
    state = absorb(fresh(q), q, own, pos, core, first_pos, rows)
    attended = finish(absorb(state, q, mate, pos, 1 - core, first_pos, rows))
    for g in range(out.shape[1] // HD):
        out[:, g * HD : (g + 1) * HD] = attended[g * rows : (g + 1) * rows]


def second_layer(half, place, scaled, inverse, pos, own, mate, near, far):
    return pl.pallas_call(
        functools.partial(second_layer_kernel, half),
        out_shape=jax.ShapeDtypeStruct((scaled.shape[1], near.shape[2]), jnp.bfloat16),
        in_specs=[SMEM_SPEC] + [VMEM_SPEC] * 7,
        out_specs=VMEM_SPEC,
        compiler_params=limit(28),
        name="second_layer",
    )(place, scaled, inverse, pos, own, in_vmem(mate), in_hbm(near), in_hbm(far))


def per_device(
    self_hidden, kv_weight, signs, positions, queries, out_weight, query_weight, norm_gain
):
    rows, width = self_hidden.shape
    sections, ctxs, heads = (lax.axis_size(a) for a in ("section", "ctx", "head"))
    section, ctx, head = (lax.axis_index(a) for a in ("section", "ctx", "head"))
    share = width // heads
    depth = width // sections

    def swap_core(value):
        return lax.ppermute(value, "section", [(i, i ^ 1) for i in range(sections)])

    def swap_y(value):
        return lax.ppermute(value, "section", [(i, i ^ 2) for i in range(sections)])

    def swap_far_y(value):
        pairs = [
            (s * heads + h, (s ^ 2) * heads + (h ^ 1))
            for s in range(sections)
            for h in range(heads)
        ]
        return lax.ppermute(value, ("section", "head"), pairs)

    def columns(of):
        return lax.dynamic_slice_in_dim(self_hidden, of * depth, depth, 1)

    here = section.reshape(1)
    first_pos = lax.dynamic_index_in_dim(positions, (section * ctxs + ctx) * rows, 0, False)
    place = jnp.stack([section, first_pos])
    pos = positions.reshape(2, sections // 2, ctxs, rows)
    pos = jnp.transpose(pos, (1, 2, 0, 3)).reshape(sections, ctxs * rows)

    def pair(value):
        groups = [[i, i + 1] for i in range(0, sections, 2)]
        return lax.all_gather(value, "section", axis=0, axis_index_groups=groups)

    near_columns = columns(section ^ 2)
    far_columns = columns(section ^ 3)
    from_near = swap_y(near_columns)
    from_far = swap_far_y(far_columns)
    near_columns, far_columns, moved_weight = lax.optimization_barrier(
        (near_columns, far_columns, kv_weight)
    )
    mate_weight = swap_core(moved_weight)
    own = kv_own(here, self_hidden, kv_weight, mate_weight)
    own, send = kv_near(own, from_near, from_far, kv_weight, mate_weight)
    other = swap_y(send)
    out_all = lax.all_gather(out_weight, "section", axis=0)
    query_near = pair(query_weight)
    send, moved_query = lax.optimization_barrier((send, query_weight))
    query_far = swap_y(moved_query)
    gain = norm_gain.astype(jnp.float32)
    own_gain = lax.dynamic_slice_in_dim(gain, head * share, share, 0).reshape(1, share)
    inverse = (1.0 / gain).reshape(heads, share)
    other, place, pos, own_gain, inverse = lax.optimization_barrier(
        (other, place, pos, own_gain, inverse)
    )
    turned = rotate(here, signs, own, other).astype(jnp.float16)
    coded = lax.all_gather(turned, "ctx", axis=0)
    coded, query_far = lax.optimization_barrier((coded, query_far))
    coded = coded.astype(jnp.float32)
    power = coded[:, 2 * rows : 2 * rows + 1]
    cache_own = (coded[:, : 2 * rows] * jnp.exp2(power - TOP)).astype(jnp.bfloat16)
    cache_own = cache_own.reshape(ctxs * 2 * rows, KV)
    cache_mate = swap_core(cache_own)
    state = own_keys(place, queries, pos, cache_own)
    partial = first_layer(0, place, queries, pos, cache_mate, state, out_all, heads)
    partial, late_hidden, query_far = lax.optimization_barrier((partial, self_hidden, query_far))
    own_hidden = lax.dynamic_slice_in_dim(late_hidden, head * share, share, 1)
    pieces = lax.all_to_all(partial, "head", 0, 0, tiled=True)
    query_far = pair(query_far)
    stream, spread = residual_sum(pieces, own_hidden, own_gain)
    scaled_all = lax.all_to_all(spread, "head", 0, 0, tiled=True)
    second = second_layer(
        0, place, scaled_all, inverse, pos, cache_own, cache_mate, query_near, query_far
    )
    return (stream, second)


def solution(mesh):
    return jax.shard_map(
        per_device,
        mesh=mesh,
        in_specs=(
            P(("section", "ctx"), None),
            P("section", "head"),
            P("head", None),
            P(),
            P(("section", "ctx"), "head"),
            P("head", "section"),
            P("section", "head"),
            P(),
        ),
        out_specs=(P(("section", "ctx"), "head"), P(("section", "ctx"), "head")),
        check_vma=False,
    )
```
